128 devices in a mesh: row: 8 (over z, y_lo), col: 16 (over x, y_hi, core).
Axes of the slice: x: 4, y: 4 (y_hi: 2, y_lo: 2; y = y_hi * 2 + y_lo), z: 4, core: 2. Of those that a mesh axis runs over, the one named last changes fastest.
Arguments:
- activations: bfloat16 [2048, 12288], P('col', 'row'), may hold values from -45 to 45
- qkv_weight: bfloat16 [12288, 3, 12288], P('row', None, 'col'), may hold values from -0.108253175 to 0.108253175
- out_weight: bfloat16 [12288, 12288], P('col', 'row'), may hold values from -0.21875 to 0.21875
Outputs:
- attn_out: bfloat16 [2048, 12288], P('col', 'row')
The draws below stay inside these ranges and needn't reach their ends.
All inputs are finite; a program needn't handle non-finite values.
Results may differ from the reference program's by a relative error of at most 0.012.
The reference program's roundings to bfloat16 on the way (of `normed`, `projected` and `attended`) count: a program that leaves them out, or rounds other values in their place, can miss the bound.
Values may be sent and summed in bfloat16 or wider, within the bound.
A program may use at most 128 MiB of HBM per device.

```python
import math
import jax
import jax.numpy as jnp
from jax import lax

D = 12288
HEADS = 96
HEAD_DIM = 128
SEQ = 2048


def shared_parts(key):
    ramp = 1.0 + 2.0 * jnp.arange(D, dtype=jnp.float32) / (D - 1)
    rough = jnp.exp(jax.random.uniform(jax.random.fold_in(key, 92), (D,), jnp.float32) * math.log(10.0))
    column_scale = ramp * rough / 10.0
    return column_scale


def draw_activations(key, part):
    column_scale = shared_parts(key)
    base = jnp.clip(jax.random.normal(jax.random.fold_in(key, 14), (SEQ, D), jnp.float32), -5.0, 5.0)
    values = base * column_scale[None, :]
    return values.astype(jnp.bfloat16)


def draw_qkv_weight(key, part):
    spread = 1.0 / math.sqrt(D)
    query_weight = jnp.clip(jax.random.normal(jax.random.fold_in(key, 25), (D, D), jnp.float32), -4.0, 4.0) * spread
    key_weight = jnp.clip(jax.random.normal(jax.random.fold_in(key, 26), (D, D), jnp.float32), -4.0, 4.0) * spread
    value_weight = jnp.clip(jax.random.normal(jax.random.fold_in(key, 27), (D, D), jnp.float32), -4.0, 4.0) * spread
    return jnp.stack([query_weight, key_weight, value_weight], axis=1).astype(jnp.bfloat16)


def levels(own_key, shape, shards, smallest, largest):
    loudness = 1.0
    for axis_at, blocks in shards:
        heights = jax.random.uniform(jax.random.fold_in(jax.random.fold_in(own_key, 6), axis_at), (blocks,), jnp.float32, smallest / len(shards), largest / len(shards))
        loudness = loudness * jnp.repeat(jnp.exp(heights), shape[axis_at] // blocks).reshape((-1,) + (1,) * (len(shape) - 1 - axis_at))
    return loudness


def scatter_about(own_key, extent, deviation, bound, split=(), held_as=jnp.bfloat16):
    factor_of = levels(own_key, extent, split, -0.22, 0.18) if split else 1.0
    values = jax.random.normal(own_key, extent, jnp.float32) * deviation * factor_of
    return jnp.minimum(jnp.maximum(values, -bound), bound).astype(held_as)


def setup_inputs(seed: int = 0) -> dict:
    key_list = jax.random.split(jax.random.key(seed), 4)
    activations = draw_activations(jax.random.fold_in(key_list[3], 71), 0)
    qkv_weight = draw_qkv_weight(jax.random.fold_in(key_list[3], 71), 0)
    out_weight = scatter_about(key_list[2], (D, D), (D // 16) ** -0.5, 0.21875, ((0, 16), (1, 8)))
    return {"activations": activations, "qkv_weight": qkv_weight, "out_weight": out_weight}


epsilon = 1e-05

def layer_normed(widened, totals, squares):
    average = totals / D
    variance = squares / D - average * average
    return ((widened - average[:, None]) * lax.rsqrt(variance + epsilon)[:, None]).astype(jnp.bfloat16)

def reference(activations, qkv_weight, out_weight):
    widened = activations.astype(jnp.float32)
    totals = lax.optimization_barrier(jnp.sum(widened, 1))
    squares = lax.optimization_barrier(jnp.sum(widened * widened, 1))
    normed = layer_normed(widened, totals, squares)
    projected = jnp.dot(normed, qkv_weight.reshape(D, 3 * D), preferred_element_type=jnp.float32).astype(jnp.bfloat16)
    seq_total = activations.shape[0]
    positions = jnp.arange(seq_total, dtype=jnp.int32)
    allowed = positions[:, None] >= positions[None, :]
    score_scale = 1.0 / HEAD_DIM ** 0.5

    def one_head(head):
        offset = (head * HEAD_DIM).astype(jnp.int32)
        queries = lax.dynamic_slice_in_dim(projected, offset, HEAD_DIM, 1)
        key_part = lax.dynamic_slice_in_dim(projected, offset + D, HEAD_DIM, 1)
        value_part = lax.dynamic_slice_in_dim(projected, offset + 2 * D, HEAD_DIM, 1)
        scores = jnp.dot(queries, key_part.T, preferred_element_type=jnp.float32) * score_scale
        scores = jnp.where(allowed, scores, jnp.float32(-1e+30))
        row_max = lax.optimization_barrier(jnp.max(scores, 1))
        weights = jnp.where(allowed, jnp.exp(scores - row_max[:, None]), jnp.float32(0.0))
        denominator = lax.optimization_barrier(jnp.sum(weights, 1))
        mixed = jnp.dot(weights.astype(jnp.bfloat16), value_part, preferred_element_type=jnp.float32)
        return (mixed / denominator[:, None]).astype(jnp.bfloat16)
    per_head = lax.map(one_head, jnp.arange(HEADS, dtype=jnp.int32))
    attended = per_head.transpose(1, 0, 2).reshape(seq_total, D)
    summed = jnp.dot(attended, out_weight, preferred_element_type=jnp.float32)
    return summed.astype(jnp.bfloat16)
```

```python
import functools

import jax
import jax.numpy as jnp
from jax import lax
from jax.experimental import pallas as pl
from jax.experimental.pallas import tpu as pltpu
from jax.sharding import PartitionSpec as P

D = 12288
HEAD_DIM = 128
EPSILON = 1e-05
MESH = pl.DeviceIdType.MESH
F32 = jnp.float32
BF16 = jnp.bfloat16

ARRIVAL = ((0, 0), (0, 1), (1, 0), (3, 0), (2, 0), (1, 1), (3, 1), (2, 1))
Z_FIRST = (True, False, True, False, True, False, True, True)
DEPART = ((2, 1), (2, 0), (1, 1), (3, 1), (1, 0), (3, 0), (0, 1), (0, 0))
SPREAD_Z_FIRST = (True, False, True, False, True, False, True, False)
OTHERS = tuple((dz, dy) for dz in range(4) for dy in range(2) if (dz, dy) != (0, 0))


class Place:
    def __init__(self):
        row = lax.axis_index("row")
        col = lax.axis_index("col")
        self.z, self.y = row // 2, row % 2
        self.x, self.yh, self.core = col // 4, (col // 2) % 2, col % 2

    def device(self, dz=0, dy=0, dx=0, dyh=0, dcore=0):
        row = ((self.z + dz) % 4) * 2 + (self.y + dy) % 2
        col = ((self.x + dx) % 4) * 4 + ((self.yh + dyh) % 2) * 2 + (self.core + dcore) % 2
        return {"row": row, "col": col}

    def level(self, dz):
        return (self.z + dz + 2 * self.core) % 4

    def active(self, dz):
        return self.level(dz) < 3

    def head(self, dz, dy):
        return self.level(dz) * 2 + (self.y + dy) % 2

    def chunk(self, dx, dyh):
        return ((self.x + dx) % 4) * 2 + (self.yh + dyh) % 2


class Traffic:
    def __init__(self, place):
        self.place = place
        self.sent = []

    def send(self, build, level=None):
        def make():
            src, dst, send_sem, recv_sem, target = build()
            return pltpu.make_async_remote_copy(
                src_ref=src,
                dst_ref=dst,
                send_sem=send_sem,
                recv_sem=recv_sem,
                device_id=target,
                device_id_type=MESH,
            )

        make().start()
        self.sent.append((make, level))

    def arrive(self, dst, send_sem, recv_sem):
        pltpu.make_async_remote_copy(
            src_ref=dst,
            dst_ref=dst,
            send_sem=send_sem,
            recv_sem=recv_sem,
            device_id=self.place.device(dcore=1),
            device_id_type=MESH,
        ).wait_recv()

    def drain(self):
        for make, level in self.sent:
            if level is None:
                make().wait_send()
            else:
                pl.when(self.place.active(level))(lambda make=make: make().wait_send())


def greet(place):
    barrier = pltpu.get_barrier_semaphore()
    peers = [place.device(dz=dz, dy=dy) for dz, dy in OTHERS]
    peers += [place.device(dcore=1), place.device(dyh=1)]
    peers += [place.device(dx=dx) for dx in (1, 2, 3)]
    for peer in peers:
        pl.semaphore_signal(barrier, inc=1, device_id=peer, device_id_type=MESH)
    return barrier, len(peers)


def row_tiles(count, tile, body):
    def step(i, carry):
        body(pl.ds(pl.multiple_of(i * tile, tile), tile))
        return carry

    lax.fori_loop(0, count // tile, step, 0)


def project_kernel(
    act_ref, w_ref, qkv_ref,
    wv, nb, pb, yr, ca, zb, st,
    w_sem, st_s, st_r, ag_s, ag_r, y_s, y_r, a_s, a_r, b_s, b_r,
):
    place = Place()
    z, y, core = place.z, place.y, place.core
    traffic = Traffic(place)
    loads = [pltpu.make_async_copy(w_ref.at[k], wv.at[k], w_sem.at[k]) for k in range(3)]
    for load in loads:
        load.start()
    barrier, greeted = greet(place)

    wide = act_ref[...].astype(F32)
    total = jnp.sum(wide, 1, keepdims=True)
    square = jnp.sum(wide * wide, 1, keepdims=True)
    lane = lax.broadcasted_iota(jnp.int32, (128, 128), 1)
    st[0] = jnp.where(lane == 0, total, square).T[0:8]
    pl.semaphore_wait(barrier, greeted)
    for dz, dy in OTHERS:
        slot = ((4 - dz) % 4) * 2 + dy
        traffic.send(
            lambda slot=slot, dz=dz, dy=dy: (
                st.at[0], st.at[slot], st_s.at[slot], st_r.at[slot], place.device(dz=dz, dy=dy)
            )
        )
    for slot in range(1, 8):
        traffic.arrive(st.at[slot], st_s.at[slot], st_r.at[slot])
    sums = st[0]
    for slot in range(1, 8):
        sums = sums + st[slot]
    turned = jnp.concatenate([sums] * 16, axis=0).T
    average = turned[:, 0:1] / D
    variance = turned[:, 1:2] / D - average * average
    scale = lax.rsqrt(variance + EPSILON)
    nb[0, 0, core] = ((act_ref[...].astype(F32) - average) * scale).astype(BF16)

    used = []

    def share(dx, dyh, ex, eyh, ecore):
        rx, ryh, count = (dx - ex) % 4, (dyh + eyh) % 2, len(used)
        traffic.send(
            lambda: (
                nb.at[dx, dyh, core],
                nb.at[rx, ryh, core],
                ag_s.at[count],
                ag_r.at[rx, ryh, core],
                place.device(dx=ex, dyh=eyh, dcore=ecore),
            )
        )
        used.append(0)

    share(0, 0, 0, 0, 1)
    share(0, 0, 0, 1, 0)
    for ex in (1, 3, 2):
        share(0, 0, ex, 0, 0)

    def receive(dx, dyh, of):
        traffic.arrive(nb.at[dx, dyh, of], ag_s.at[0], ag_r.at[dx, dyh, of])

    def stage_gather(step):
        dx, dyh = ARRIVAL[step]
        if step:
            receive(dx, dyh, core)
            share(dx, dyh, 0, 0, 1)
            if (dx, dyh) == (0, 1):
                for ex in (1, 3, 2):
                    share(0, 1, ex, 0, 0)
        receive(dx, dyh, 1 - core)

    def stage_project(step):
        dx, dyh = ARRIVAL[step]

        def tile(i, carry):
            kind, level = i // 3, i % 3
            columns = pl.ds(pl.multiple_of(level * 256, 256), 256)
            part = jnp.dot(
                nb[dx, dyh].reshape(256, 1536), wv[kind, :, columns], preferred_element_type=F32
            ).astype(BF16)
            dz = (level + 8 - 2 * core - z) % 4
            where = pl.ds(pl.multiple_of(kind * 128, 128), 128)
            for side in range(2):
                pb[step, dz, (side + y) % 2, :, where] = part[:, side * 128 : side * 128 + 128]
            return carry

        lax.fori_loop(0, 9, tile, 0)

    def sides(step):
        return pl.ds(0, 2 if Z_FIRST[step] else 1)

    def send_y(step, dz):
        traffic.send(
            lambda: (
                pb.at[step, dz, 1], yr.at[step, dz], y_s.at[step, dz], y_r.at[step, dz],
                place.device(dy=1),
            ),
            dz,
        )

    def arrive_y(step, dz):
        traffic.arrive(yr.at[step, dz], y_s.at[step, dz], y_r.at[step, dz])

    def z_far(step):
        def go():
            for way, hop in ((0, 1), (1, 3)):
                traffic.send(
                    lambda way=way, hop=hop: (
                        pb.at[step, 2, sides(step), pl.ds(way * 128, 128)],
                        ca.at[step, way, sides(step)],
                        a_s.at[step, way],
                        a_r.at[step, way],
                        place.device(dz=hop),
                    ),
                    2,
                )

        pl.when(place.active(2))(go)

    def z_near(step):
        for way, hop in ((0, 1), (1, 3)):

            def go(way=way, hop=hop):
                traffic.arrive(ca.at[step, way, sides(step)], a_s.at[step, way], a_r.at[step, way])
                for side in range(2 if Z_FIRST[step] else 1):

                    def add(rows, side=side):
                        at = pl.ds(pl.multiple_of(rows.start + way * 128, 32), 32)
                        pb[step, hop, side, at, :] = (
                            pb[step, hop, side, at, :].astype(F32)
                            + ca[step, way, side, rows, :].astype(F32)
                        ).astype(BF16)

                    row_tiles(128, 32, add)
                traffic.send(
                    lambda: (
                        pb.at[step, hop, sides(step)], zb.at[step, way, sides(step)],
                        b_s.at[step, way], b_r.at[step, way], place.device(dz=hop),
                    ),
                    hop,
                )

            pl.when(place.active(hop))(go)

    def arrive_near(step):
        for way in range(2):
            traffic.arrive(zb.at[step, way, sides(step)], b_s.at[step, way], b_r.at[step, way])

    def finish(step):
        t = place.chunk(*ARRIVAL[step])

        def add(rows):
            at = pl.ds(pl.multiple_of(rows.start + t * 256, 32), 32)
            qkv_ref[at, :] = (
                pb[step, 0, 0, rows, :].astype(F32)
                + yr[step, 0, rows, :].astype(F32)
                + zb[step, 0, 0, rows, :].astype(F32)
                + zb[step, 1, 0, rows, :].astype(F32)
            ).astype(BF16)

        row_tiles(256, 32, add)

    def stage_a(step):
        stage_gather(step)
        if step == 0:
            for load in loads:
                load.wait()
        stage_project(step)
        if Z_FIRST[step]:
            z_far(step)
        else:
            for dz in (2, 1, 3, 0):
                pl.when(place.active(dz))(functools.partial(send_y, step, dz))

    def stage_b(step):
        if Z_FIRST[step]:
            z_near(step)
            return
        for dz in (2, 1, 3):

            def go(dz=dz):
                arrive_y(step, dz)

                def add(rows):
                    pb[step, dz, 0, rows, :] = (
                        pb[step, dz, 0, rows, :].astype(F32) + yr[step, dz, rows, :].astype(F32)
                    ).astype(BF16)

                row_tiles(256, 32, add)

            pl.when(place.active(dz))(go)
            if dz == 2:
                z_far(step)

    def stage_c(step):
        if not Z_FIRST[step]:
            z_near(step)
            return

        def go():
            arrive_near(step)

            def add(rows):
                pb[step, 0, 1, rows, :] = (
                    pb[step, 0, 1, rows, :].astype(F32)
                    + zb[step, 0, 1, rows, :].astype(F32)
                    + zb[step, 1, 1, rows, :].astype(F32)
                ).astype(BF16)

            row_tiles(256, 32, add)
            send_y(step, 0)

        pl.when(place.active(0))(go)

    def stage_d(step):
        def go():
            if not Z_FIRST[step]:
                arrive_near(step)
            arrive_y(step, 0)
            finish(step)

        pl.when(place.active(0))(go)

    for turn in range(11):
        for lag, stage in enumerate((stage_a, stage_b, stage_c, stage_d)):
            if 0 <= turn - lag < 8:
                stage(turn - lag)
    traffic.drain()


def attend_kernel(
    qkv_ref, wo_ref, out_ref,
    wv, at, score, acc, cs, cr, pb, ca, xb, yr,
    w_sem, t_s, t_r, c_s, c_r, a_s, a_r, b_s, b_r, y_s, y_r,
):
    place = Place()
    core = place.core
    traffic = Traffic(place)
    load = pltpu.make_async_copy(wo_ref, wv, w_sem)
    load.start()
    barrier, greeted = greet(place)
    pl.semaphore_wait(barrier, greeted)
    factor = 1.4426950408889634 / HEAD_DIM**0.5

    def head_columns(dz, dy):
        return pl.ds(pl.multiple_of(place.head(dz, dy) * 128, 128), 128)

    def piece(step, dz, dy):
        return at.at[step, :, head_columns(dz, dy)]

    def attend(step):
        t = place.chunk(*DEPART[step])
        query = qkv_ref[pl.ds(pl.multiple_of(t * 256, 256), 256), 0:128]

        def block(j):
            return pl.ds(pl.multiple_of(j * 256, 256), 256)

        def scores(j):
            return lax.dot_general(
                query, qkv_ref[block(j), 128:256], (((1,), (1,)), ((), ())),
                preferred_element_type=F32,
            )

        def first(j, top):
            now = scores(j)
            score[:, block(j)] = now
            return jnp.maximum(top, jnp.maximum(now[:, :128], now[:, 128:]))

        row = lax.broadcasted_iota(jnp.int32, (256, 256), 0)
        col = lax.broadcasted_iota(jnp.int32, (256, 256), 1)
        now = jnp.where(row >= col, scores(t), F32(-1e30))
        score[:, block(t)] = now
        top = lax.fori_loop(0, t, first, jnp.maximum(now[:, :128], now[:, 128:]))
        top = jnp.max(top, 1, keepdims=True)

        def second(j, state):
            low, mixed = state
            weight = jnp.exp2((score[:, block(j)] - top) * factor)
            low = low + (weight[:, :128] + weight[:, 128:])
            mixed = mixed + jnp.dot(
                weight.astype(BF16), qkv_ref[block(j), 256:384], preferred_element_type=F32
            )
            return low, mixed

        zero = jnp.zeros((256, 128), F32)
        low, mixed = lax.fori_loop(0, t + 1, second, (zero, zero))
        at[step, :, head_columns(0, 0)] = (mixed / jnp.sum(low, 1, keepdims=True)).astype(BF16)

    spread = []

    def share(step, dz, dy, ez, ey):
        rz, ry = (dz - ez) % 4, (dy + ey) % 2
        count = sum(1 for s in spread if s == step)
        spread.append(step)
        traffic.send(
            lambda: (
                piece(step, dz, dy), piece(step, dz, dy), t_s.at[step, count],
                t_r.at[step, rz, ry], place.device(dz=ez, dy=ey),
            ),
            dz,
        )

    def receive(step, dz, dy):
        traffic.arrive(piece(step, dz, dy), t_s.at[step, 0], t_r.at[step, dz, dy])

    def stage_a(step):
        def go():
            attend(step)
            share(step, 0, 0, 0, 1)
            for ez in (2, 1, 3):
                share(step, 0, 0, ez, 0)

        pl.when(place.active(0))(go)

    def stage_b(step):
        if SPREAD_Z_FIRST[step]:
            for dz in (1, 3, 2):

                def go(dz=dz):
                    receive(step, dz, 0)
                    share(step, dz, 0, 0, 1)

                pl.when(place.active(dz))(go)
        else:

            def go():
                receive(step, 0, 1)
                for ez in (2, 1, 3):
                    share(step, 0, 1, ez, 0)

            pl.when(place.active(0))(go)

    def stage_c(step):
        if step == 0:
            load.wait()
        for dz, dy in OTHERS:
            done = dy == 0 and dz > 0 if SPREAD_Z_FIRST[step] else (dz, dy) == (0, 1)
            if not done:
                pl.when(place.active(dz))(functools.partial(receive, step, dz, dy))

        def half(which):
            return at[step, pl.ds(pl.multiple_of(which * 128, 128), 128), :]

        def theirs(i, carry):
            columns = pl.ds(pl.multiple_of(i * 256, 256), 256)
            cs[step, :, columns] = jnp.dot(
                half(1 - core), wv[:, columns], preferred_element_type=F32
            ).astype(BF16)
            return carry

        lax.fori_loop(0, 6, theirs, 0)
        traffic.send(
            lambda: (cs.at[step], cr.at[step], c_s.at[step], c_r.at[step], place.device(dcore=1))
        )

        def mine(i, carry):
            columns = pl.ds(pl.multiple_of(i * 256, 256), 256)
            acc[step % 2, :, columns] = jnp.dot(
                half(core), wv[:, columns], preferred_element_type=F32
            )
            return carry

        lax.fori_loop(0, 6, mine, 0)

    def stage_d(step):
        dx, dyh = DEPART[step]
        traffic.arrive(cr.at[step], c_s.at[step], c_r.at[step])
        way = {1: 0, 3: 1}.get(dx)
        if way is not None:
            traffic.arrive(ca.at[dyh, way], a_s.at[dyh, way], a_r.at[dyh, way])
        if dx == 0:
            for w in range(2):
                traffic.arrive(xb.at[dyh, w], b_s.at[dyh, w], b_r.at[dyh, w])
            if dyh == 0:
                traffic.arrive(yr, y_s, y_r)

        def combine(lo):
            def add(rows):
                here = pl.ds(pl.multiple_of(rows.start + lo * 64, 16), 16)
                now = acc[step % 2, here, :] + cr[step, here, :].astype(F32)
                if way is not None and lo == way:
                    now = now + ca[dyh, way, rows, :].astype(F32)
                if dx == 0:
                    now = now + xb[dyh, 0, here, :].astype(F32) + xb[dyh, 1, here, :].astype(F32)
                if (dx, dyh) == (0, 0):
                    out_ref[here, :] = (now + yr[here, :].astype(F32)).astype(BF16)
                else:
                    pb[dx, dyh, here, :] = now.astype(BF16)

            row_tiles(64, 16, add)

        combine(0)
        combine(1)
        if dx == 2:
            for w, hop in ((0, 1), (1, 3)):
                traffic.send(
                    lambda w=w, hop=hop: (
                        pb.at[2, dyh, pl.ds(w * 64, 64)], ca.at[dyh, w], a_s.at[dyh, w],
                        a_r.at[dyh, w], place.device(dx=hop),
                    )
                )
        elif way is not None:
            traffic.send(
                lambda: (
                    pb.at[dx, dyh], xb.at[dyh, way], b_s.at[dyh, way], b_r.at[dyh, way],
                    place.device(dx=dx),
                )
            )
        elif dyh == 1:
            traffic.send(lambda: (pb.at[0, 1], yr, y_s, y_r, place.device(dyh=1)))

    for turn in range(11):
        for lag, stage in enumerate((stage_a, stage_b, stage_c, stage_d)):
            if 0 <= turn - lag < 8:
                stage(turn - lag)
    traffic.drain()


def dma(*shape):
    return pltpu.SemaphoreType.DMA(shape) if shape else pltpu.SemaphoreType.DMA


def project(activations, weight):
    return pl.pallas_call(
        project_kernel,
        out_shape=jax.ShapeDtypeStruct((2048, 384), BF16),
        in_specs=[pl.BlockSpec(memory_space=pltpu.VMEM), pl.BlockSpec(memory_space=pl.ANY)],
        out_specs=pl.BlockSpec(memory_space=pltpu.VMEM),
        scratch_shapes=[
            pltpu.VMEM((3, 1536, 768), BF16),
            pltpu.VMEM((4, 2, 2, 128, 1536), BF16),
            pltpu.VMEM((8, 4, 2, 256, 384), BF16),
            pltpu.VMEM((8, 4, 256, 384), BF16),
            pltpu.VMEM((8, 2, 2, 128, 384), BF16),
            pltpu.VMEM((8, 2, 2, 256, 384), BF16),
            pltpu.VMEM((8, 8, 128), F32),
            dma(3), dma(8), dma(8), dma(16), dma(4, 2, 2), dma(8, 4), dma(8, 4),
            dma(8, 2), dma(8, 2), dma(8, 2), dma(8, 2),
        ],
        compiler_params=pltpu.CompilerParams(
            collective_id=1, has_side_effects=True, vmem_limit_bytes=56 << 20
        ),
        name="project",
    )(activations, weight)


def attend(qkv, weight):
    return pl.pallas_call(
        attend_kernel,
        out_shape=jax.ShapeDtypeStruct((128, 1536), BF16),
        in_specs=[pl.BlockSpec(memory_space=pltpu.VMEM), pl.BlockSpec(memory_space=pl.ANY)],
        out_specs=pl.BlockSpec(memory_space=pltpu.VMEM),
        scratch_shapes=[
            pltpu.VMEM((768, 1536), BF16),
            pltpu.VMEM((8, 256, 768), BF16),
            pltpu.VMEM((256, 2048), F32),
            pltpu.VMEM((2, 128, 1536), F32),
            pltpu.VMEM((8, 128, 1536), BF16),
            pltpu.VMEM((8, 128, 1536), BF16),
            pltpu.VMEM((4, 2, 128, 1536), BF16),
            pltpu.VMEM((2, 2, 64, 1536), BF16),
            pltpu.VMEM((2, 2, 128, 1536), BF16),
            pltpu.VMEM((128, 1536), BF16),
            dma(), dma(8, 8), dma(8, 4, 2), dma(8), dma(8),
            dma(2, 2), dma(2, 2), dma(2, 2), dma(2, 2), dma(), dma(),
        ],
        compiler_params=pltpu.CompilerParams(
            collective_id=2, has_side_effects=True, vmem_limit_bytes=56 << 20
        ),
        name="attend",
    )(qkv, weight)


def per_device(activations, qkv_weight, out_weight):
    qkv = project(activations, jnp.transpose(qkv_weight, (1, 0, 2)))
    return attend(qkv, out_weight)


def solution(mesh):
    in_specs = (P("col", "row"), P("row", None, "col"), P("col", "row"))
    return jax.shard_map(
        per_device, mesh=mesh, in_specs=in_specs, out_specs=P("col", "row"), check_vma=False
    )
```

```python
import functools

import jax
import jax.numpy as jnp
from jax import lax
from jax.experimental import pallas as pl
from jax.experimental.pallas import tpu as pltpu
from jax.sharding import PartitionSpec as P

D = 12288
HEAD_DIM = 128
EPSILON = 1e-05
MESH = pl.DeviceIdType.MESH
F32 = jnp.float32
BF16 = jnp.bfloat16

ARRIVAL = ((0, 0), (0, 1), (1, 0), (3, 0), (2, 0), (1, 1), (3, 1), (2, 1))
PROJECT_LAGS = (0, 1, 2, 3)
ATTEND_LAGS = (0, 1, 2, 3, 4)
ZY = (0, 128, 64)
YZ = (128, 128, 64)
DEPART = ((2, 1), (1, 1), (3, 1), (2, 0), (0, 1), (1, 0), (3, 0), (0, 0))
SPREAD_Z_FIRST = (True, False, True, False, True, False, True, False)
OTHERS = tuple((dz, dy) for dz in range(4) for dy in range(2) if (dz, dy) != (0, 0))


class Place:
    def __init__(self):
        row = lax.axis_index("row")
        col = lax.axis_index("col")
        self.z, self.y = row // 2, row % 2
        self.x, self.yh, self.core = col // 4, (col // 2) % 2, col % 2

    def device(self, dz=0, dy=0, dx=0, dyh=0, dcore=0):
        row = ((self.z + dz) % 4) * 2 + (self.y + dy) % 2
        col = ((self.x + dx) % 4) * 4 + ((self.yh + dyh) % 2) * 2 + (self.core + dcore) % 2
        return {"row": row, "col": col}

    def level(self, dz):
        return (self.z + dz + 2 * self.core) % 4

    def active(self, dz):
        return self.level(dz) < 3

    def head(self, dz, dy):
        return self.level(dz) * 2 + (self.y + dy) % 2

    def chunk(self, dx, dyh):
        return ((self.x + dx) % 4) * 2 + (self.yh + dyh) % 2


class Traffic:
    def __init__(self, place):
        self.place = place
        self.sent = []

    def send(self, build, level=None):
        def make():
            src, dst, send_sem, recv_sem, target = build()
            return pltpu.make_async_remote_copy(
                src_ref=src,
                dst_ref=dst,
                send_sem=send_sem,
                recv_sem=recv_sem,
                device_id=target,
                device_id_type=MESH,
            )

        make().start()
        self.sent.append((make, level))

    def arrive(self, dst, send_sem, recv_sem):
        pltpu.make_async_remote_copy(
            src_ref=dst,
            dst_ref=dst,
            send_sem=send_sem,
            recv_sem=recv_sem,
            device_id=self.place.device(dcore=1),
            device_id_type=MESH,
        ).wait_recv()

    def drain(self):
        for make, level in self.sent:
            if level is None:
                make().wait_send()
            else:
                pl.when(self.place.active(level))(lambda make=make: make().wait_send())


def greet(place):
    barrier = pltpu.get_barrier_semaphore()
    peers = [place.device(dz=dz, dy=dy) for dz, dy in OTHERS]
    peers += [place.device(dcore=1), place.device(dyh=1)]
    peers += [place.device(dx=dx) for dx in (1, 2, 3)]
    for peer in peers:
        pl.semaphore_signal(barrier, inc=1, device_id=peer, device_id_type=MESH)
    return barrier, len(peers)


def row_tiles(count, tile, body):
    def step(i, carry):
        body(pl.ds(pl.multiple_of(i * tile, tile), tile))
        return carry

    lax.fori_loop(0, count // tile, step, 0)


def schedule(lags, stages, opening=()):
    done = set()
    order = list(opening)
    for turn in range(8 + max(lags)):
        order += [(i, turn - lag) for i, lag in enumerate(lags) if 0 <= turn - lag < 8]
    for i, step in order:
        if (i, step) not in done:
            done.add((i, step))
            stages[i](step)


def project(
    place, traffic, act_ref, w_ref, wo_ref, wov, qkv,
    wv, nb, pb, yrz, yry, caz, cay, zbz, zby, st,
    w_sem, st_s, st_r, ag_s, ag_r, yz_s, yz_r, y_s, y_r, a_s, a_r, b_s, b_r,
):
    z, y, core = place.z, place.y, place.core
    loads = [pltpu.make_async_copy(w_ref.at[k], wv.at[k], w_sem.at[k]) for k in range(3)]
    out_load = pltpu.make_async_copy(wo_ref, wov, w_sem.at[3])
    for load in [*loads, out_load]:
        load.start()
    barrier, greeted = greet(place)

    wide = act_ref[...].astype(F32)
    total = jnp.sum(wide, 1, keepdims=True)
    square = jnp.sum(wide * wide, 1, keepdims=True)
    lane = lax.broadcasted_iota(jnp.int32, (128, 128), 1)
    st[0] = jnp.where(lane == 0, total, square).T[0:8]
    pl.semaphore_wait(barrier, greeted)
    for dz, dy in OTHERS:
        slot = ((4 - dz) % 4) * 2 + dy
        traffic.send(
            lambda slot=slot, dz=dz, dy=dy: (
                st.at[0], st.at[slot], st_s.at[slot], st_r.at[slot], place.device(dz=dz, dy=dy)
            )
        )
    for slot in range(1, 8):
        traffic.arrive(st.at[slot], st_s.at[slot], st_r.at[slot])
    sums = st[0]
    for slot in range(1, 8):
        sums = sums + st[slot]
    turned = jnp.concatenate([sums] * 16, axis=0).T
    average = turned[:, 0:1] / D
    variance = turned[:, 1:2] / D - average * average
    scale = lax.rsqrt(variance + EPSILON)
    nb[0, 0, core] = ((act_ref[...].astype(F32) - average) * scale).astype(BF16)

    used = []

    def share(dx, dyh, ex, eyh, ecore):
        rx, ryh, count = (dx - ex) % 4, (dyh + eyh) % 2, len(used)
        traffic.send(
            lambda: (
                nb.at[dx, dyh, core],
                nb.at[rx, ryh, core],
                ag_s.at[count],
                ag_r.at[rx, ryh, core],
                place.device(dx=ex, dyh=eyh, dcore=ecore),
            )
        )
        used.append(0)

    share(0, 0, 0, 1, 0)
    for ex in (1, 3):
        share(0, 0, ex, 0, 0)
    share(0, 0, 0, 0, 1)

    def relay(dyh):
        count = len(used)
        traffic.send(
            lambda: (
                nb.at[3 - 2 * core, dyh, core],
                nb.at[2, dyh, core],
                ag_s.at[count],
                ag_r.at[2, dyh, core],
                place.device(dx=1 + 2 * core),
            )
        )
        used.append(0)

    def receive(dx, dyh, of):
        traffic.arrive(nb.at[dx, dyh, of], ag_s.at[0], ag_r.at[dx, dyh, of])

    def stage_gather(step):
        dx, dyh = ARRIVAL[step]
        if step:
            receive(dx, dyh, core)
            if (dx, dyh) == (0, 1):
                for ex in (1, 3):
                    share(0, 1, ex, 0, 0)
            if dx == 3:
                relay(dyh)
            share(dx, dyh, 0, 0, 1)
        receive(dx, dyh, 1 - core)

    def stage_project(step):
        dx, dyh = ARRIVAL[step]

        def tile(i, carry):
            kind, level = i // 3, i % 3
            columns = pl.ds(pl.multiple_of(level * 256, 256), 256)
            part = jnp.dot(
                nb[dx, dyh].reshape(256, 1536), wv[kind, :, columns], preferred_element_type=F32
            ).astype(BF16)
            dz = (level + 8 - 2 * core - z) % 4
            where = pl.ds(pl.multiple_of(kind * 128, 128), 128)
            for side in range(2):
                pb[step, dz, (side + y) % 2, :, where] = part[:, side * 128 : side * 128 + 128]
            return carry

        lax.fori_loop(0, 9, tile, 0)

    def rows_of(part, way):
        low, count, first = part
        return pl.ds(low, first) if way == 0 else pl.ds(low + first, count - first)

    def z_far(part, step):
        both = part is ZY
        for way, hop in ((0, 1), (1, 3)):
            rows = rows_of(part, way)
            into = pl.ds(0, rows.size)
            traffic.send(
                lambda way=way, hop=hop, rows=rows, into=into: (
                    pb.at[step, 2, :, rows] if both else pb.at[step, 2, 0, rows],
                    caz.at[step, way, :, into] if both else cay.at[step, way, into],
                    a_s.at[int(both), step, way],
                    a_r.at[int(both), step, way],
                    place.device(dz=hop),
                ),
                2,
            )

    def z_near(part, step):
        both = part is ZY
        for way, hop in ((0, 1), (1, 3)):

            def go(way=way, hop=hop):
                rows = rows_of(part, way)
                into = pl.ds(0, rows.size)
                traffic.arrive(
                    caz.at[step, way, :, into] if both else cay.at[step, way, into],
                    a_s.at[int(both), step, way],
                    a_r.at[int(both), step, way],
                )
                for side in range(2 if both else 1):

                    def add(tile, side=side):
                        here = pl.ds(pl.multiple_of(tile.start + rows.start, 16), 16)
                        far = caz[step, way, side, tile, :] if both else cay[step, way, tile, :]
                        pb[step, hop, side, here, :] = (
                            pb[step, hop, side, here, :].astype(F32) + far.astype(F32)
                        ).astype(BF16)

                    row_tiles(rows.size, 16, add)
                whole = pl.ds(part[0], part[1])
                traffic.send(
                    lambda: (
                        pb.at[step, hop, :, whole] if both else pb.at[step, hop, 0, whole],
                        zbz.at[step, way] if both else zby.at[step, way],
                        b_s.at[int(both), step, way],
                        b_r.at[int(both), step, way],
                        place.device(dz=hop),
                    ),
                    hop,
                )

            pl.when(place.active(hop))(go)

    def arrive_near(part, step):
        both = part is ZY
        for way in range(2):
            traffic.arrive(
                zbz.at[step, way] if both else zby.at[step, way],
                b_s.at[int(both), step, way],
                b_r.at[int(both), step, way],
            )

    def send_y(step, dz):
        traffic.send(
            lambda: (
                pb.at[step, dz, 1, pl.ds(YZ[0], YZ[1])], yry.at[step, dz], y_s.at[step, dz],
                y_r.at[step, dz], place.device(dy=1),
            ),
            dz,
        )

    def stage_a(step):
        stage_gather(step)
        if step == 0:
            for load in loads:
                load.wait()
        stage_project(step)
        pl.when(place.active(2))(functools.partial(z_far, ZY, step))
        for dz in (2, 1, 3, 0):
            pl.when(place.active(dz))(functools.partial(send_y, step, dz))

    def stage_b(step):
        z_near(ZY, step)
        for dz in (2, 1, 3):

            def go(dz=dz):
                traffic.arrive(yry.at[step, dz], y_s.at[step, dz], y_r.at[step, dz])

                def add(tile):
                    here = pl.ds(pl.multiple_of(tile.start + YZ[0], 16), 16)
                    pb[step, dz, 0, here, :] = (
                        pb[step, dz, 0, here, :].astype(F32) + yry[step, dz, tile, :].astype(F32)
                    ).astype(BF16)

                row_tiles(YZ[1], 16, add)
                if dz == 2:
                    z_far(YZ, step)

            pl.when(place.active(dz))(go)

    def stage_c(step):
        z_near(YZ, step)

        def go():
            arrive_near(ZY, step)

            def add(tile):
                pb[step, 0, 1, tile, :] = (
                    pb[step, 0, 1, tile, :].astype(F32)
                    + zbz[step, 0, 1, tile, :].astype(F32)
                    + zbz[step, 1, 1, tile, :].astype(F32)
                ).astype(BF16)

            row_tiles(ZY[1], 16, add)
            traffic.send(
                lambda: (
                    pb.at[step, 0, 1, pl.ds(ZY[0], ZY[1])], yrz.at[step], yz_s.at[step],
                    yz_r.at[step], place.device(dy=1),
                ),
                0,
            )

        pl.when(place.active(0))(go)

    def stage_d(step):
        t = place.chunk(*ARRIVAL[step])

        def go():
            arrive_near(YZ, step)
            traffic.arrive(yry.at[step, 0], y_s.at[step, 0], y_r.at[step, 0])
            traffic.arrive(yrz.at[step], yz_s.at[step], yz_r.at[step])

            def finish(low, yr, zb0, zb1):
                def add(tile):
                    mine = pl.ds(pl.multiple_of(tile.start + low, 16), 16)
                    here = pl.ds(pl.multiple_of(tile.start + low + t * 256, 16), 16)
                    qkv[here, :] = (
                        pb[step, 0, 0, mine, :].astype(F32)
                        + yr[tile, :].astype(F32)
                        + zb0[tile, :].astype(F32)
                        + zb1[tile, :].astype(F32)
                    ).astype(BF16)

                return add

            row_tiles(
                ZY[1], 16, finish(ZY[0], yrz.at[step], zbz.at[step, 0, 0], zbz.at[step, 1, 0])
            )
            row_tiles(
                YZ[1], 16, finish(YZ[0], yry.at[step, 0], zby.at[step, 0], zby.at[step, 1])
            )

        pl.when(place.active(0))(go)

    schedule(PROJECT_LAGS, (stage_a, stage_b, stage_c, stage_d))
    return out_load


def attend_all(
    place, traffic, out_load, qkv_ref, out_ref,
    wv, at, score, acc, cs, cr, pb, ca, xb, yr,
    t_s, t_r, c_s, c_r, a_s, a_r, b_s, b_r, y_s, y_r,
):
    core = place.core
    factor = 1.4426950408889634 / HEAD_DIM**0.5

    def head_columns(dz, dy):
        return pl.ds(pl.multiple_of(place.head(dz, dy) * 128, 128), 128)

    def piece(step, dz, dy):
        return at.at[step, :, head_columns(dz, dy)]

    def attend(step):
        t = place.chunk(*DEPART[step])
        query = qkv_ref[pl.ds(pl.multiple_of(t * 256, 256), 256), 0:128]

        def block(j):
            return pl.ds(pl.multiple_of(j * 256, 256), 256)

        def scores(j):
            return lax.dot_general(
                query, qkv_ref[block(j), 128:256], (((1,), (1,)), ((), ())),
                preferred_element_type=F32,
            )

        def first(j, top):
            now = scores(j)
            score[:, block(j)] = now
            return jnp.maximum(top, jnp.maximum(now[:, :128], now[:, 128:]))

        row = lax.broadcasted_iota(jnp.int32, (256, 256), 0)
        col = lax.broadcasted_iota(jnp.int32, (256, 256), 1)
        now = jnp.where(row >= col, scores(t), F32(-1e30))
        score[:, block(t)] = now
        top = lax.fori_loop(0, t, first, jnp.maximum(now[:, :128], now[:, 128:]))
        top = jnp.max(top, 1, keepdims=True)

        def second(j, state):
            low, mixed = state
            weight = jnp.exp2((score[:, block(j)] - top) * factor)
            low = low + (weight[:, :128] + weight[:, 128:])
            mixed = mixed + jnp.dot(
                weight.astype(BF16), qkv_ref[block(j), 256:384], preferred_element_type=F32
            )
            return low, mixed

        zero = jnp.zeros((256, 128), F32)
        low, mixed = lax.fori_loop(0, t + 1, second, (zero, zero))
        at[step, :, head_columns(0, 0)] = (mixed / jnp.sum(low, 1, keepdims=True)).astype(BF16)

    spread = []

    def share(step, dz, dy, ez, ey):
        rz, ry = (dz - ez) % 4, (dy + ey) % 2
        count = sum(1 for s in spread if s == step)
        spread.append(step)
        traffic.send(
            lambda: (
                piece(step, dz, dy), piece(step, dz, dy), t_s.at[step, count],
                t_r.at[step, rz, ry], place.device(dz=ez, dy=ey),
            ),
            dz,
        )

    def receive(step, dz, dy):
        traffic.arrive(piece(step, dz, dy), t_s.at[step, 0], t_r.at[step, dz, dy])

    def relay(step):
        return 1 if (step // 2) % 2 == 0 else 3

    def stage_a(step):
        def go():
            attend(step)
            for ez, ey in ((1, 0), (3, 0), (0, 1)):
                share(step, 0, 0, ez, ey)

        pl.when(place.active(0))(go)

    def stage_b(step):
        onward = relay(step)
        if SPREAD_Z_FIRST[step]:
            for dz in (4 - onward, onward):

                def go(dz=dz):
                    receive(step, dz, 0)
                    if dz == 4 - onward:
                        share(step, dz, 0, onward, 0)
                    share(step, dz, 0, 0, 1)

                pl.when(place.active(dz))(go)
        else:

            def go():
                receive(step, 0, 1)
                for ez in (1, 3):
                    share(step, 0, 1, ez, 0)

            pl.when(place.active(0))(go)

    def stage_c(step):
        onward = relay(step)
        if SPREAD_Z_FIRST[step]:

            def go():
                receive(step, 2, 0)
                share(step, 2, 0, 0, 1)

            pl.when(place.active(2))(go)
        else:

            def go():
                for dy in range(2):
                    receive(step, 4 - onward, dy)
                    share(step, 4 - onward, dy, onward, 0)

            pl.when(place.active(4 - onward))(go)

    def stage_d(step):
        if step == 0:
            out_load.wait()
        for dz, dy in OTHERS:
            if SPREAD_Z_FIRST[step]:
                done = dy == 0
            else:
                done = dz == 4 - relay(step) or (dz, dy) == (0, 1)
            if not done:
                pl.when(place.active(dz))(functools.partial(receive, step, dz, dy))

        def half(which):
            return at[step, pl.ds(pl.multiple_of(which * 128, 128), 128), :]

        def theirs(i, carry):
            columns = pl.ds(pl.multiple_of(i * 256, 256), 256)
            cs[step, :, columns] = jnp.dot(
                half(1 - core), wv[:, columns], preferred_element_type=F32
            ).astype(BF16)
            return carry

        lax.fori_loop(0, 6, theirs, 0)
        traffic.send(
            lambda: (cs.at[step], cr.at[step], c_s.at[step], c_r.at[step], place.device(dcore=1))
        )

        def mine(i, carry):
            columns = pl.ds(pl.multiple_of(i * 256, 256), 256)
            acc[step % 2, :, columns] = jnp.dot(
                half(core), wv[:, columns], preferred_element_type=F32
            )
            return carry

        lax.fori_loop(0, 6, mine, 0)

    def stage_e(step):
        dx, dyh = DEPART[step]
        traffic.arrive(cr.at[step], c_s.at[step], c_r.at[step])
        way = {1: 0, 3: 1}.get(dx)
        if way is not None:
            traffic.arrive(ca.at[dyh, way], a_s.at[dyh, way], a_r.at[dyh, way])
        if dx == 0:
            for w in range(2):
                traffic.arrive(xb.at[dyh, w], b_s.at[dyh, w], b_r.at[dyh, w])
            if dyh == 0:
                traffic.arrive(yr, y_s, y_r)

        def combine(lo):
            def add(rows):
                here = pl.ds(pl.multiple_of(rows.start + lo * 64, 16), 16)
                now = acc[step % 2, here, :] + cr[step, here, :].astype(F32)
                if way is not None and lo == way:
                    now = now + ca[dyh, way, rows, :].astype(F32)
                if dx == 0:
                    now = now + xb[dyh, 0, here, :].astype(F32) + xb[dyh, 1, here, :].astype(F32)
                if (dx, dyh) == (0, 0):
                    out_ref[here, :] = (now + yr[here, :].astype(F32)).astype(BF16)
                else:
                    pb[dx, dyh, here, :] = now.astype(BF16)

            row_tiles(64, 16, add)

        combine(0)
        combine(1)
        if dx == 2:
            for w, hop in ((0, 1), (1, 3)):
                traffic.send(
                    lambda w=w, hop=hop: (
                        pb.at[2, dyh, pl.ds(w * 64, 64)], ca.at[dyh, w], a_s.at[dyh, w],
                        a_r.at[dyh, w], place.device(dx=hop),
                    )
                )
        elif way is not None:
            traffic.send(
                lambda: (
                    pb.at[dx, dyh], xb.at[dyh, way], b_s.at[dyh, way], b_r.at[dyh, way],
                    place.device(dx=dx),
                )
            )
        elif dyh == 1:
            traffic.send(lambda: (pb.at[0, 1], yr, y_s, y_r, place.device(dyh=1)))

    schedule(ATTEND_LAGS, (stage_a, stage_b, stage_c, stage_d, stage_e))


def block_kernel(act_ref, w_ref, wo_ref, out_ref, qkv, wov, *scratch):
    place = Place()
    traffic = Traffic(place)
    cut = len(PROJECT_SCRATCH)
    out_load = project(place, traffic, act_ref, w_ref, wo_ref, wov, qkv, *scratch[:cut])
    attend_all(place, traffic, out_load, qkv, out_ref, wov, *scratch[cut:])
    traffic.drain()


def dma(*shape):
    return pltpu.SemaphoreType.DMA(shape) if shape else pltpu.SemaphoreType.DMA


PROJECT_SCRATCH = (
    pltpu.VMEM((3, 1536, 768), BF16),
    pltpu.VMEM((4, 2, 2, 128, 1536), BF16),
    pltpu.VMEM((8, 4, 2, 256, 384), BF16),
    pltpu.VMEM((8, ZY[1], 384), BF16),
    pltpu.VMEM((8, 4, YZ[1], 384), BF16),
    pltpu.VMEM((8, 2, 2, ZY[2], 384), BF16),
    pltpu.VMEM((8, 2, YZ[2], 384), BF16),
    pltpu.VMEM((8, 2, 2, ZY[1], 384), BF16),
    pltpu.VMEM((8, 2, YZ[1], 384), BF16),
    pltpu.VMEM((8, 8, 128), F32),
    dma(4), dma(8), dma(8), dma(16), dma(4, 2, 2), dma(8), dma(8), dma(8, 4), dma(8, 4),
    dma(2, 8, 2), dma(2, 8, 2), dma(2, 8, 2), dma(2, 8, 2),
)
ATTEND_SCRATCH = (
    pltpu.VMEM((8, 256, 768), BF16),
    pltpu.VMEM((256, 2048), F32),
    pltpu.VMEM((2, 128, 1536), F32),
    pltpu.VMEM((8, 128, 1536), BF16),
    pltpu.VMEM((8, 128, 1536), BF16),
    pltpu.VMEM((4, 2, 128, 1536), BF16),
    pltpu.VMEM((2, 2, 64, 1536), BF16),
    pltpu.VMEM((2, 2, 128, 1536), BF16),
    pltpu.VMEM((128, 1536), BF16),
    dma(8, 8), dma(8, 4, 2), dma(8), dma(8),
    dma(2, 2), dma(2, 2), dma(2, 2), dma(2, 2), dma(), dma(),
)


def per_device(activations, qkv_weight, out_weight):
    return pl.pallas_call(
        block_kernel,
        out_shape=jax.ShapeDtypeStruct((128, 1536), BF16),
        in_specs=[
            pl.BlockSpec(memory_space=pltpu.VMEM),
            pl.BlockSpec(memory_space=pl.ANY),
            pl.BlockSpec(memory_space=pl.ANY),
        ],
        out_specs=pl.BlockSpec(memory_space=pltpu.VMEM),
        scratch_shapes=[
            pltpu.VMEM((2048, 384), BF16),
            pltpu.VMEM((768, 1536), BF16),
            *PROJECT_SCRATCH,
            *ATTEND_SCRATCH,
        ],
        compiler_params=pltpu.CompilerParams(
            collective_id=1, has_side_effects=True, vmem_limit_bytes=60 << 20
        ),
        name="block",
    )(activations, jnp.transpose(qkv_weight, (1, 0, 2)), out_weight)


def solution(mesh):
    in_specs = (P("col", "row"), P("row", None, "col"), P("col", "row"))
    return jax.shard_map(
        per_device, mesh=mesh, in_specs=in_specs, out_specs=P("col", "row"), check_vma=False
    )
```

```python
import functools

import jax
import jax.numpy as jnp
from jax import lax
from jax.experimental import pallas as pl
from jax.experimental.pallas import tpu as pltpu
from jax.sharding import PartitionSpec as P

D = 12288
HEAD_DIM = 128
EPSILON = 1e-05
MESH = pl.DeviceIdType.MESH
F32 = jnp.float32
BF16 = jnp.bfloat16

ARRIVAL = ((0, 0), (0, 1), (1, 0), (3, 0), (2, 0), (1, 1), (3, 1), (2, 1))
PROJECT_LAGS = (0, 1, 2, 3)
ATTEND_LAGS = (0, 1, 2, 3, 4)
ZY = (0, 128, 64)
YZ = (128, 128, 64)
DEPART = ((2, 1), (1, 1), (3, 1), (2, 0), (0, 1), (1, 0), (3, 0), (0, 0))
SPREAD_Z_FIRST = (True, False, True, False, True, False, True, False)
OTHERS = tuple((dz, dy) for dz in range(4) for dy in range(2) if (dz, dy) != (0, 0))


class Place:
    def __init__(self):
        row = lax.axis_index("row")
        col = lax.axis_index("col")
        self.z, self.y = row // 2, row % 2
        self.x, self.yh, self.core = col // 4, (col // 2) % 2, col % 2

    def device(self, dz=0, dy=0, dx=0, dyh=0, dcore=0):
        row = ((self.z + dz) % 4) * 2 + (self.y + dy) % 2
        col = ((self.x + dx) % 4) * 4 + ((self.yh + dyh) % 2) * 2 + (self.core + dcore) % 2
        return {"row": row, "col": col}

    def level(self, dz):
        return (self.z + dz + 2 * self.core) % 4

    def active(self, dz):
        return self.level(dz) < 3

    def head(self, dz, dy):
        return self.level(dz) * 2 + (self.y + dy) % 2

    def chunk(self, dx, dyh):
        return ((self.x + dx) % 4) * 2 + (self.yh + dyh) % 2


class Traffic:
    def __init__(self, place):
        self.place = place
        self.sent = []

    def send(self, build, level=None):
        def make():
            src, dst, send_sem, recv_sem, target = build()
            return pltpu.make_async_remote_copy(
                src_ref=src,
                dst_ref=dst,
                send_sem=send_sem,
                recv_sem=recv_sem,
                device_id=target,
                device_id_type=MESH,
            )

        make().start()
        self.sent.append((make, level))

    def arrive(self, dst, send_sem, recv_sem):
        pltpu.make_async_remote_copy(
            src_ref=dst,
            dst_ref=dst,
            send_sem=send_sem,
            recv_sem=recv_sem,
            device_id=self.place.device(dcore=1),
            device_id_type=MESH,
        ).wait_recv()

    def drain(self):
        for make, level in self.sent:
            if level is None:
                make().wait_send()
            else:
                pl.when(self.place.active(level))(lambda make=make: make().wait_send())


def greet(place):
    barrier = pltpu.get_barrier_semaphore()
    peers = [place.device(dz=dz, dy=dy) for dz, dy in OTHERS]
    peers += [place.device(dcore=1), place.device(dyh=1)]
    peers += [place.device(dx=dx) for dx in (1, 2, 3)]
    for peer in peers:
        pl.semaphore_signal(barrier, inc=1, device_id=peer, device_id_type=MESH)
    return barrier, len(peers)


def row_tiles(count, tile, body):
    def step(i, carry):
        body(pl.ds(pl.multiple_of(i * tile, tile), tile))
        return carry

    lax.fori_loop(0, count // tile, step, 0)


def schedule(lags, stages, opening=()):
    done = set()
    order = list(opening)
    for turn in range(8 + max(lags)):
        order += [(i, turn - lag) for i, lag in enumerate(lags) if 0 <= turn - lag < 8]
    for i, step in order:
        if (i, step) not in done:
            done.add((i, step))
            stages[i](step)


def project(
    place, traffic, act_ref, w_ref, wo_ref, wov, qkv,
    wv, nb, pb, yrz, yry, caz, cay, zbz, zby, st,
    w_sem, st_s, st_r, ag_s, ag_r, yz_s, yz_r, y_s, y_r, a_s, a_r, b_s, b_r,
):
    z, y, core = place.z, place.y, place.core
    loads = [pltpu.make_async_copy(w_ref.at[k], wv.at[k], w_sem.at[k]) for k in range(3)]
    out_load = pltpu.make_async_copy(wo_ref, wov, w_sem.at[3])
    for load in [*loads, out_load]:
        load.start()
    barrier, greeted = greet(place)

    wide = act_ref[...].astype(F32)
    total = jnp.sum(wide, 1, keepdims=True)
    square = jnp.sum(wide * wide, 1, keepdims=True)
    lane = lax.broadcasted_iota(jnp.int32, (128, 128), 1)
    st[0] = jnp.where(lane == 0, total, square).T[0:8]
    pl.semaphore_wait(barrier, greeted)
    for dz, dy in OTHERS:
        slot = ((4 - dz) % 4) * 2 + dy
        traffic.send(
            lambda slot=slot, dz=dz, dy=dy: (
                st.at[0], st.at[slot], st_s.at[slot], st_r.at[slot], place.device(dz=dz, dy=dy)
            )
        )
    for slot in range(1, 8):
        traffic.arrive(st.at[slot], st_s.at[slot], st_r.at[slot])
    sums = st[0]
    for slot in range(1, 8):
        sums = sums + st[slot]
    turned = jnp.concatenate([sums] * 16, axis=0).T
    average = turned[:, 0:1] / D
    variance = turned[:, 1:2] / D - average * average
    scale = lax.rsqrt(variance + EPSILON)
    nb[0, 0, core] = ((act_ref[...].astype(F32) - average) * scale).astype(BF16)

    used = []

    def share(dx, dyh, ex, eyh, ecore):
        rx, ryh, count = (dx - ex) % 4, (dyh + eyh) % 2, len(used)
        traffic.send(
            lambda: (
                nb.at[dx, dyh, core],
                nb.at[rx, ryh, core],
                ag_s.at[count],
                ag_r.at[rx, ryh, core],
                place.device(dx=ex, dyh=eyh, dcore=ecore),
            )
        )
        used.append(0)

    share(0, 0, 0, 1, 0)
    for ex in (1, 3):
        share(0, 0, ex, 0, 0)
    share(0, 0, 0, 0, 1)

    def relay(dyh):
        count = len(used)
        traffic.send(
            lambda: (
                nb.at[3 - 2 * core, dyh, core],
                nb.at[2, dyh, core],
                ag_s.at[count],
                ag_r.at[2, dyh, core],
                place.device(dx=1 + 2 * core),
            )
        )
        used.append(0)

    def receive(dx, dyh, of):
        traffic.arrive(nb.at[dx, dyh, of], ag_s.at[0], ag_r.at[dx, dyh, of])

    def stage_gather(step):
        dx, dyh = ARRIVAL[step]
        if step:
            receive(dx, dyh, core)
            if (dx, dyh) == (0, 1):
                for ex in (1, 3):
                    share(0, 1, ex, 0, 0)
            if dx == 3:
                relay(dyh)
            share(dx, dyh, 0, 0, 1)
        receive(dx, dyh, 1 - core)

    def stage_project(step):
        dx, dyh = ARRIVAL[step]

        def tile(kind, carry):
            part = jnp.dot(
                nb[dx, dyh].reshape(256, 1536), wv[kind], preferred_element_type=F32
            ).astype(BF16)
            where = pl.ds(pl.multiple_of(kind * 128, 128), 128)
            for head in range(6):
                dz = (head // 2 + 8 - 2 * core - z) % 4
                pb[step, dz, (head + y) % 2, :, where] = part[:, head * 128 : head * 128 + 128]
            return carry

        lax.fori_loop(0, 3, tile, 0)

    def rows_of(part, way):
        low, count, first = part
        return pl.ds(low, first) if way == 0 else pl.ds(low + first, count - first)

    def z_far(part, step):
        both = part is ZY
        for way, hop in ((0, 1), (1, 3)):
            rows = rows_of(part, way)
            into = pl.ds(0, rows.size)
            traffic.send(
                lambda way=way, hop=hop, rows=rows, into=into: (
                    pb.at[step, 2, :, rows] if both else pb.at[step, 2, 0, rows],
                    caz.at[step, way, :, into] if both else cay.at[step, way, into],
                    a_s.at[int(both), step, way],
                    a_r.at[int(both), step, way],
                    place.device(dz=hop),
                ),
                2,
            )

    def near(part, step, way, half):
        rows = rows_of(part, half)
        into = pl.ds(rows.start - part[0], rows.size)
        return rows, zbz.at[step, way, :, into] if part is ZY else zby.at[step, way, into]

    def send_near(part, step, way, half):
        both, hop = part is ZY, 1 + 2 * way

        def build():
            rows, into = near(part, step, way, half)
            return (
                pb.at[step, hop, :, rows] if both else pb.at[step, hop, 0, rows],
                into,
                b_s.at[int(both), step, way, half],
                b_r.at[int(both), step, way, half],
                place.device(dz=hop),
            )

        traffic.send(build, hop)

    def z_alone(part, step, way):
        pl.when(place.active(1 + 2 * way))(lambda: send_near(part, step, way, 1 - way))

    def z_near(part, step):
        both = part is ZY
        for way, hop in ((0, 1), (1, 3)):

            def go(way=way, hop=hop):
                rows = rows_of(part, way)
                into = pl.ds(0, rows.size)
                traffic.arrive(
                    caz.at[step, way, :, into] if both else cay.at[step, way, into],
                    a_s.at[int(both), step, way],
                    a_r.at[int(both), step, way],
                )
                for side in range(2 if both else 1):

                    def add(tile, side=side):
                        here = pl.ds(pl.multiple_of(tile.start + rows.start, 16), tile.size)
                        far = caz[step, way, side, tile, :] if both else cay[step, way, tile, :]
                        pb[step, hop, side, here, :] = (
                            pb[step, hop, side, here, :].astype(F32) + far.astype(F32)
                        ).astype(BF16)

                    row_tiles(rows.size, 64, add)
                send_near(part, step, way, way)

            pl.when(place.active(hop))(go)

    def arrive_near(part, step):
        both = part is ZY
        for way in range(2):
            for half in range(2):
                traffic.arrive(
                    near(part, step, way, half)[1],
                    b_s.at[int(both), step, way, half],
                    b_r.at[int(both), step, way, half],
                )

    def send_y(step, dz):
        traffic.send(
            lambda: (
                pb.at[step, dz, 1, pl.ds(YZ[0], YZ[1])], yry.at[step, dz], y_s.at[step, dz],
                y_r.at[step, dz], place.device(dy=1),
            ),
            dz,
        )

    def stage_a(step):
        stage_gather(step)
        if step == 0:
            for load in loads:
                load.wait()
        stage_project(step)
        pl.when(place.active(2))(functools.partial(z_far, ZY, step))
        for dz in (2, 1, 3, 0):
            pl.when(place.active(dz))(functools.partial(send_y, step, dz))
        for way in range(2):
            z_alone(ZY, step, way)

    def stage_b(step):
        z_near(ZY, step)
        for dz in (2, 1, 3):

            def go(dz=dz):
                traffic.arrive(yry.at[step, dz], y_s.at[step, dz], y_r.at[step, dz])

                def add(tile):
                    here = pl.ds(pl.multiple_of(tile.start + YZ[0], 16), tile.size)
                    pb[step, dz, 0, here, :] = (
                        pb[step, dz, 0, here, :].astype(F32) + yry[step, dz, tile, :].astype(F32)
                    ).astype(BF16)

                row_tiles(YZ[1], 64, add)
                if dz == 2:
                    z_far(YZ, step)

            pl.when(place.active(dz))(go)
            if dz != 2:
                z_alone(YZ, step, dz // 2)

    def stage_c(step):
        z_near(YZ, step)

        def go():
            arrive_near(ZY, step)

            def add(tile):
                pb[step, 0, 1, tile, :] = (
                    pb[step, 0, 1, tile, :].astype(F32)
                    + zbz[step, 0, 1, tile, :].astype(F32)
                    + zbz[step, 1, 1, tile, :].astype(F32)
                ).astype(BF16)

            row_tiles(ZY[1], 64, add)
            traffic.send(
                lambda: (
                    pb.at[step, 0, 1, pl.ds(ZY[0], ZY[1])], yrz.at[step], yz_s.at[step],
                    yz_r.at[step], place.device(dy=1),
                ),
                0,
            )

        pl.when(place.active(0))(go)

    def stage_d(step):
        t = place.chunk(*ARRIVAL[step])

        def go():
            arrive_near(YZ, step)
            traffic.arrive(yry.at[step, 0], y_s.at[step, 0], y_r.at[step, 0])
            traffic.arrive(yrz.at[step], yz_s.at[step], yz_r.at[step])

            def finish(low, yr, zb0, zb1):
                def add(tile):
                    mine = pl.ds(pl.multiple_of(tile.start + low, 16), tile.size)
                    here = pl.ds(pl.multiple_of(tile.start + low + t * 256, 16), tile.size)
                    qkv[here, :] = (
                        pb[step, 0, 0, mine, :].astype(F32)
                        + yr[tile, :].astype(F32)
                        + zb0[tile, :].astype(F32)
                        + zb1[tile, :].astype(F32)
                    ).astype(BF16)

                return add

            row_tiles(
                ZY[1], 64, finish(ZY[0], yrz.at[step], zbz.at[step, 0, 0], zbz.at[step, 1, 0])
            )
            row_tiles(
                YZ[1], 64, finish(YZ[0], yry.at[step, 0], zby.at[step, 0], zby.at[step, 1])
            )

        pl.when(place.active(0))(go)

    schedule(PROJECT_LAGS, (stage_a, stage_b, stage_c, stage_d))
    return out_load


def attend_all(
    place, traffic, out_load, qkv_ref, out_ref,
    wv, at, score, acc, cs, cr, pb, ca, xb, yr,
    t_s, t_r, c_s, c_r, a_s, a_r, b_s, b_r, y_s, y_r,
):
    core = place.core
    factor = 1.4426950408889634 / HEAD_DIM**0.5

    def head_columns(dz, dy):
        return pl.ds(pl.multiple_of(place.head(dz, dy) * 128, 128), 128)

    def piece(step, dz, dy):
        return at.at[step, :, head_columns(dz, dy)]

    def attend(step):
        t = place.chunk(*DEPART[step])
        last = t // 2
        query = qkv_ref[pl.ds(pl.multiple_of(t * 256, 256), 256), 0:128]

        def block(j):
            return pl.ds(pl.multiple_of(j * 512, 512), 512)

        def scores(j):
            return lax.dot_general(
                query, qkv_ref[block(j), 128:256], (((1,), (1,)), ((), ())),
                preferred_element_type=F32,
            )

        def fold(op, wide):
            return op(op(wide[:, :128], wide[:, 128:256]), op(wide[:, 256:384], wide[:, 384:]))

        def first(j, top):
            now = scores(j)
            score[:, block(j)] = now
            return jnp.maximum(top, fold(jnp.maximum, now))

        row = lax.broadcasted_iota(jnp.int32, (256, 512), 0)
        col = lax.broadcasted_iota(jnp.int32, (256, 512), 1)
        now = jnp.where(row + (t % 2) * 256 >= col, scores(last), F32(-1e30))
        score[:, block(last)] = now
        top = lax.fori_loop(0, last, first, fold(jnp.maximum, now))
        top = jnp.max(top, 1, keepdims=True)

        def second(j, state):
            low, mixed = state
            weight = jnp.exp2((score[:, block(j)] - top) * factor)
            low = low + fold(jnp.add, weight)
            mixed = mixed + jnp.dot(
                weight.astype(BF16), qkv_ref[block(j), 256:384], preferred_element_type=F32
            )
            return low, mixed

        zero = jnp.zeros((256, 128), F32)
        low, mixed = lax.fori_loop(0, last + 1, second, (zero, zero))
        at[step, :, head_columns(0, 0)] = (mixed / jnp.sum(low, 1, keepdims=True)).astype(BF16)

    spread = []

    def share(step, dz, dy, ez, ey):
        rz, ry = (dz - ez) % 4, (dy + ey) % 2
        count = sum(1 for s in spread if s == step)
        spread.append(step)
        traffic.send(
            lambda: (
                piece(step, dz, dy), piece(step, dz, dy), t_s.at[step, count],
                t_r.at[step, rz, ry], place.device(dz=ez, dy=ey),
            ),
            dz,
        )

    def receive(step, dz, dy):
        traffic.arrive(piece(step, dz, dy), t_s.at[step, 0], t_r.at[step, dz, dy])

    def relay(step):
        return 1 if (step // 2) % 2 == 0 else 3

    def stage_a(step):
        def go():
            attend(step)
            for ez, ey in ((1, 0), (3, 0), (0, 1)):
                share(step, 0, 0, ez, ey)

        pl.when(place.active(0))(go)

    def stage_b(step):
        onward = relay(step)
        if SPREAD_Z_FIRST[step]:
            for dz in (4 - onward, onward):

                def go(dz=dz):
                    receive(step, dz, 0)
                    if dz == 4 - onward:
                        share(step, dz, 0, onward, 0)
                    share(step, dz, 0, 0, 1)

                pl.when(place.active(dz))(go)
        else:

            def go():
                receive(step, 0, 1)
                for ez in (1, 3):
                    share(step, 0, 1, ez, 0)

            pl.when(place.active(0))(go)

    def stage_c(step):
        onward = relay(step)
        if SPREAD_Z_FIRST[step]:

            def go():
                receive(step, 2, 0)
                share(step, 2, 0, 0, 1)

            pl.when(place.active(2))(go)
        else:

            def go():
                for dy in range(2):
                    receive(step, 4 - onward, dy)
                    share(step, 4 - onward, dy, onward, 0)

            pl.when(place.active(4 - onward))(go)

    def stage_d(step):
        if step == 0:
            out_load.wait()
        for dz, dy in OTHERS:
            if SPREAD_Z_FIRST[step]:
                done = dy == 0
            else:
                done = dz == 4 - relay(step) or (dz, dy) == (0, 1)
            if not done:
                pl.when(place.active(dz))(functools.partial(receive, step, dz, dy))

        def half(which):
            return pl.ds(pl.multiple_of(which * 128, 128), 128)

        def tile(i, carry):
            columns = pl.ds(pl.multiple_of(i * 512, 512), 512)
            score[:, 0:512] = jnp.dot(at[step], wv[:, columns], preferred_element_type=F32)
            cs[step, :, columns] = score[half(1 - core), 0:512].astype(BF16)
            acc[step % 2, :, columns] = score[half(core), 0:512]
            return carry

        lax.fori_loop(0, 3, tile, 0)
        traffic.send(
            lambda: (cs.at[step], cr.at[step], c_s.at[step], c_r.at[step], place.device(dcore=1))
        )

    def stage_e(step):
        dx, dyh = DEPART[step]
        traffic.arrive(cr.at[step], c_s.at[step], c_r.at[step])
        way = {1: 0, 3: 1}.get(dx)
        if way is not None:
            traffic.arrive(ca.at[dyh, way], a_s.at[dyh, way], a_r.at[dyh, way])
        if dx == 0:
            for w in range(2):
                traffic.arrive(xb.at[dyh, w], b_s.at[dyh, w], b_r.at[dyh, w])
            if dyh == 0:
                traffic.arrive(yr, y_s, y_r)

        def combine(lo):
            def add(rows):
                here = pl.ds(pl.multiple_of(rows.start + lo * 64, 16), rows.size)
                now = acc[step % 2, here, :] + cr[step, here, :].astype(F32)
                if way is not None and lo == way:
                    now = now + ca[dyh, way, rows, :].astype(F32)
                if dx == 0:
                    now = now + xb[dyh, 0, here, :].astype(F32) + xb[dyh, 1, here, :].astype(F32)
                if (dx, dyh) == (0, 0):
                    out_ref[here, :] = (now + yr[here, :].astype(F32)).astype(BF16)
                else:
                    pb[dx, dyh, here, :] = now.astype(BF16)

            row_tiles(64, 32, add)

        combine(0)
        combine(1)
        if dx == 2:
            for w, hop in ((0, 1), (1, 3)):
                traffic.send(
                    lambda w=w, hop=hop: (
                        pb.at[2, dyh, pl.ds(w * 64, 64)], ca.at[dyh, w], a_s.at[dyh, w],
                        a_r.at[dyh, w], place.device(dx=hop),
                    )
                )
        elif way is not None:
            traffic.send(
                lambda: (
                    pb.at[dx, dyh], xb.at[dyh, way], b_s.at[dyh, way], b_r.at[dyh, way],
                    place.device(dx=dx),
                )
            )
        elif dyh == 1:
            traffic.send(lambda: (pb.at[0, 1], yr, y_s, y_r, place.device(dyh=1)))

    schedule(ATTEND_LAGS, (stage_a, stage_b, stage_c, stage_d, stage_e))


def block_kernel(act_ref, w_ref, wo_ref, out_ref, qkv, wov, *scratch):
    place = Place()
    traffic = Traffic(place)
    cut = len(PROJECT_SCRATCH)
    out_load = project(place, traffic, act_ref, w_ref, wo_ref, wov, qkv, *scratch[:cut])
    attend_all(place, traffic, out_load, qkv, out_ref, wov, *scratch[cut:])
    traffic.drain()


def dma(*shape):
    return pltpu.SemaphoreType.DMA(shape) if shape else pltpu.SemaphoreType.DMA


PROJECT_SCRATCH = (
    pltpu.VMEM((3, 1536, 768), BF16),
    pltpu.VMEM((4, 2, 2, 128, 1536), BF16),
    pltpu.VMEM((8, 4, 2, 256, 384), BF16),
    pltpu.VMEM((8, ZY[1], 384), BF16),
    pltpu.VMEM((8, 4, YZ[1], 384), BF16),
    pltpu.VMEM((8, 2, 2, ZY[2], 384), BF16),
    pltpu.VMEM((8, 2, YZ[2], 384), BF16),
    pltpu.VMEM((8, 2, 2, ZY[1], 384), BF16),
    pltpu.VMEM((8, 2, YZ[1], 384), BF16),
    pltpu.VMEM((8, 8, 128), F32),
    dma(4), dma(8), dma(8), dma(16), dma(4, 2, 2), dma(8), dma(8), dma(8, 4), dma(8, 4),
    dma(2, 8, 2), dma(2, 8, 2), dma(2, 8, 2, 2), dma(2, 8, 2, 2),
)
ATTEND_SCRATCH = (
    pltpu.VMEM((8, 256, 768), BF16),
    pltpu.VMEM((256, 2048), F32),
    pltpu.VMEM((2, 128, 1536), F32),
    pltpu.VMEM((8, 128, 1536), BF16),
    pltpu.VMEM((8, 128, 1536), BF16),
    pltpu.VMEM((4, 2, 128, 1536), BF16),
    pltpu.VMEM((2, 2, 64, 1536), BF16),
    pltpu.VMEM((2, 2, 128, 1536), BF16),
    pltpu.VMEM((128, 1536), BF16),
    dma(8, 8), dma(8, 4, 2), dma(8), dma(8),
    dma(2, 2), dma(2, 2), dma(2, 2), dma(2, 2), dma(), dma(),
)


def per_device(activations, qkv_weight, out_weight):
    return pl.pallas_call(
        block_kernel,
        out_shape=jax.ShapeDtypeStruct((128, 1536), BF16),
        in_specs=[
            pl.BlockSpec(memory_space=pltpu.VMEM),
            pl.BlockSpec(memory_space=pl.ANY),
            pl.BlockSpec(memory_space=pl.ANY),
        ],
        out_specs=pl.BlockSpec(memory_space=pltpu.VMEM),
        scratch_shapes=[
            pltpu.VMEM((2048, 384), BF16),
            pltpu.VMEM((768, 1536), BF16),
            *PROJECT_SCRATCH,
            *ATTEND_SCRATCH,
        ],
        compiler_params=pltpu.CompilerParams(
            collective_id=1, has_side_effects=True, vmem_limit_bytes=60 << 20
        ),
        name="block",
    )(activations, jnp.transpose(qkv_weight, (1, 0, 2)), out_weight)


def solution(mesh):
    in_specs = (P("col", "row"), P("row", None, "col"), P("col", "row"))
    return jax.shard_map(
        per_device, mesh=mesh, in_specs=in_specs, out_specs=P("col", "row"), check_vma=False
    )
```

```python
import functools

import jax
import jax.numpy as jnp
from jax import lax
from jax.experimental import pallas as pl
from jax.experimental.pallas import tpu as pltpu
from jax.sharding import PartitionSpec as P

D = 12288
HEAD_DIM = 128
EPSILON = 1e-05
MESH = pl.DeviceIdType.MESH
F32 = jnp.float32
BF16 = jnp.bfloat16

ARRIVAL = ((0, 0), (0, 1), (1, 0), (3, 0), (2, 0), (1, 1), (3, 1), (2, 1))
PROJECT_LAGS = (0, 1, 2, 4)
ATTEND_LAGS = (0, 1, 2, 3, 4)
ZY = (0, 128, 64)
YZ = (128, 128, 64)
DEPART = ((2, 1), (1, 1), (3, 1), (2, 0), (0, 1), (1, 0), (3, 0), (0, 0))
SPREAD_Z_FIRST = (True, False, True, False, True, False, True, False)
OTHERS = tuple((dz, dy) for dz in range(4) for dy in range(2) if (dz, dy) != (0, 0))


class Place:
    def __init__(self):
        row = lax.axis_index("row")
        col = lax.axis_index("col")
        self.z, self.y = row // 2, row % 2
        self.x, self.yh, self.core = col // 4, (col // 2) % 2, col % 2

    def device(self, dz=0, dy=0, dx=0, dyh=0, dcore=0):
        row = ((self.z + dz) % 4) * 2 + (self.y + dy) % 2
        col = ((self.x + dx) % 4) * 4 + ((self.yh + dyh) % 2) * 2 + (self.core + dcore) % 2
        return {"row": row, "col": col}

    def level(self, dz):
        return (self.z + dz + 2 * self.core) % 4

    def active(self, dz):
        return self.level(dz) < 3

    def head(self, dz, dy):
        return self.level(dz) * 2 + (self.y + dy) % 2

    def chunk(self, dx, dyh):
        return ((self.x + dx) % 4) * 2 + (self.yh + dyh) % 2


class Traffic:
    def __init__(self, place):
        self.place = place
        self.sent = []

    def send(self, build, level=None):
        def make():
            src, dst, send_sem, recv_sem, target = build()
            return pltpu.make_async_remote_copy(
                src_ref=src,
                dst_ref=dst,
                send_sem=send_sem,
                recv_sem=recv_sem,
                device_id=target,
                device_id_type=MESH,
            )

        make().start()
        self.sent.append((make, level))

    def arrive(self, dst, send_sem, recv_sem):
        pltpu.make_async_remote_copy(
            src_ref=dst,
            dst_ref=dst,
            send_sem=send_sem,
            recv_sem=recv_sem,
            device_id=self.place.device(dcore=1),
            device_id_type=MESH,
        ).wait_recv()

    def drain(self):
        for make, level in self.sent:
            if level is None:
                make().wait_send()
            else:
                pl.when(self.place.active(level))(lambda make=make: make().wait_send())


def greet(place):
    barrier = pltpu.get_barrier_semaphore()
    peers = [place.device(dz=dz, dy=dy) for dz, dy in OTHERS]
    peers += [place.device(dcore=1), place.device(dyh=1)]
    peers += [place.device(dx=dx) for dx in (1, 2, 3)]
    for peer in peers:
        pl.semaphore_signal(barrier, inc=1, device_id=peer, device_id_type=MESH)
    return barrier, len(peers)


def row_tiles(count, tile, body):
    def step(i, carry):
        body(pl.ds(pl.multiple_of(i * tile, tile), tile))
        return carry

    lax.fori_loop(0, count // tile, step, 0)


def schedule(lags, stages, opening=()):
    done = set()
    order = list(opening)
    for turn in range(8 + max(lags)):
        order += [(i, turn - lag) for i, lag in enumerate(lags) if 0 <= turn - lag < 8]
    for i, step in order:
        if (i, step) not in done:
            done.add((i, step))
            stages[i](step)


def project(
    place, traffic, act_ref, w_ref, wo_ref, wov, qkv,
    wv, nb, pb, yrz, yry, caz, cay, zbz, zby, st,
    w_sem, st_s, st_r, ag_s, ag_r, yz_s, yz_r, y_s, y_r, a_s, a_r, b_s, b_r,
):
    z, y, core = place.z, place.y, place.core
    loads = [pltpu.make_async_copy(w_ref.at[k], wv.at[k], w_sem.at[k]) for k in range(3)]
    out_load = pltpu.make_async_copy(wo_ref, wov, w_sem.at[3])
    for load in [*loads, out_load]:
        load.start()
    barrier, greeted = greet(place)

    wide = act_ref[...].astype(F32)
    total = jnp.sum(wide, 1, keepdims=True)
    square = jnp.sum(wide * wide, 1, keepdims=True)
    lane = lax.broadcasted_iota(jnp.int32, (128, 128), 1)
    st[0] = jnp.where(lane == 0, total, square).T[0:8]
    pl.semaphore_wait(barrier, greeted)
    for dz, dy in OTHERS:
        slot = ((4 - dz) % 4) * 2 + dy
        traffic.send(
            lambda slot=slot, dz=dz, dy=dy: (
                st.at[0], st.at[slot], st_s.at[slot], st_r.at[slot], place.device(dz=dz, dy=dy)
            )
        )
    for slot in range(1, 8):
        traffic.arrive(st.at[slot], st_s.at[slot], st_r.at[slot])
    sums = st[0]
    for slot in range(1, 8):
        sums = sums + st[slot]
    turned = jnp.concatenate([sums] * 16, axis=0).T
    average = turned[:, 0:1] / D
    variance = turned[:, 1:2] / D - average * average
    scale = lax.rsqrt(variance + EPSILON)
    nb[0, 0, core] = ((act_ref[...].astype(F32) - average) * scale).astype(BF16)

    used = []

    def share(dx, dyh, ex, eyh, ecore):
        rx, ryh, count = (dx - ex) % 4, (dyh + eyh) % 2, len(used)
        traffic.send(
            lambda: (
                nb.at[dx, dyh, core],
                nb.at[rx, ryh, core],
                ag_s.at[count],
                ag_r.at[rx, ryh, core],
                place.device(dx=ex, dyh=eyh, dcore=ecore),
            )
        )
        used.append(0)

    share(0, 0, 0, 1, 0)
    for ex in (1, 3):
        share(0, 0, ex, 0, 0)
    share(0, 0, 0, 0, 1)

    def relay(dyh):
        count = len(used)
        traffic.send(
            lambda: (
                nb.at[3 - 2 * core, dyh, core],
                nb.at[2, dyh, core],
                ag_s.at[count],
                ag_r.at[2, dyh, core],
                place.device(dx=1 + 2 * core),
            )
        )
        used.append(0)

    def receive(dx, dyh, of):
        traffic.arrive(nb.at[dx, dyh, of], ag_s.at[0], ag_r.at[dx, dyh, of])

    def stage_gather(step):
        dx, dyh = ARRIVAL[step]
        if step:
            receive(dx, dyh, core)
            if (dx, dyh) == (0, 1):
                for ex in (1, 3):
                    share(0, 1, ex, 0, 0)
            if dx == 3:
                relay(dyh)
            share(dx, dyh, 0, 0, 1)
        receive(dx, dyh, 1 - core)

    def stage_project(step):
        dx, dyh = ARRIVAL[step]

        def tile(kind, carry):
            part = jnp.dot(
                nb[dx, dyh].reshape(256, 1536), wv[kind], preferred_element_type=F32
            ).astype(BF16)
            where = pl.ds(pl.multiple_of(kind * 128, 128), 128)
            for head in range(6):
                dz = (head // 2 + 8 - 2 * core - z) % 4
                pb[step, dz, (head + y) % 2, :, where] = part[:, head * 128 : head * 128 + 128]
            return carry

        lax.fori_loop(0, 3, tile, 0)

    def rows_of(part, way):
        low, count, first = part
        return pl.ds(low, first) if way == 0 else pl.ds(low + first, count - first)

    def z_far(part, step):
        both = part is ZY
        for way, hop in ((0, 1), (1, 3)):
            rows = rows_of(part, way)
            into = pl.ds(0, rows.size)
            traffic.send(
                lambda way=way, hop=hop, rows=rows, into=into: (
                    pb.at[step, 2, :, rows] if both else pb.at[step, 2, 0, rows],
                    caz.at[step, way, :, into] if both else cay.at[step, way, into],
                    a_s.at[int(both), step, way],
                    a_r.at[int(both), step, way],
                    place.device(dz=hop),
                ),
                2,
            )

    def near(part, step, way, half):
        rows = rows_of(part, half)
        into = pl.ds(rows.start - part[0], rows.size)
        return rows, zbz.at[step, way, :, into] if part is ZY else zby.at[step, way, into]

    def send_near(part, step, way, half):
        both, hop = part is ZY, 1 + 2 * way

        def build():
            rows, into = near(part, step, way, half)
            return (
                pb.at[step, hop, :, rows] if both else pb.at[step, hop, 0, rows],
                into,
                b_s.at[int(both), step, way, half],
                b_r.at[int(both), step, way, half],
                place.device(dz=hop),
            )

        traffic.send(build, hop)

    def z_alone(part, step, way):
        pl.when(place.active(1 + 2 * way))(lambda: send_near(part, step, way, 1 - way))

    def z_near(part, step):
        both = part is ZY
        for way, hop in ((0, 1), (1, 3)):

            def go(way=way, hop=hop):
                rows = rows_of(part, way)
                into = pl.ds(0, rows.size)
                traffic.arrive(
                    caz.at[step, way, :, into] if both else cay.at[step, way, into],
                    a_s.at[int(both), step, way],
                    a_r.at[int(both), step, way],
                )
                for side in range(2 if both else 1):

                    def add(tile, side=side):
                        here = pl.ds(pl.multiple_of(tile.start + rows.start, 16), tile.size)
                        far = caz[step, way, side, tile, :] if both else cay[step, way, tile, :]
                        pb[step, hop, side, here, :] = (
                            pb[step, hop, side, here, :].astype(F32) + far.astype(F32)
                        ).astype(BF16)

                    row_tiles(rows.size, 64, add)
                send_near(part, step, way, way)

            pl.when(place.active(hop))(go)

    def arrive_near(part, step):
        both = part is ZY
        for way in range(2):
            for half in range(2):
                traffic.arrive(
                    near(part, step, way, half)[1],
                    b_s.at[int(both), step, way, half],
                    b_r.at[int(both), step, way, half],
                )

    def send_y(step, dz):
        traffic.send(
            lambda: (
                pb.at[step, dz, 1, pl.ds(YZ[0], YZ[1])], yry.at[step, dz], y_s.at[step, dz],
                y_r.at[step, dz], place.device(dy=1),
            ),
            dz,
        )

    def stage_a(step):
        stage_gather(step)
        if step == 0:
            for load in loads:
                load.wait()
        stage_project(step)
        pl.when(place.active(2))(functools.partial(z_far, ZY, step))
        for dz in (2, 1, 3, 0):
            pl.when(place.active(dz))(functools.partial(send_y, step, dz))
        for way in range(2):
            z_alone(ZY, step, way)

    def stage_b(step):
        z_near(ZY, step)
        for dz in (2, 1, 3):

            def go(dz=dz):
                traffic.arrive(yry.at[step, dz], y_s.at[step, dz], y_r.at[step, dz])

                def add(tile):
                    here = pl.ds(pl.multiple_of(tile.start + YZ[0], 16), tile.size)
                    pb[step, dz, 0, here, :] = (
                        pb[step, dz, 0, here, :].astype(F32) + yry[step, dz, tile, :].astype(F32)
                    ).astype(BF16)

                row_tiles(YZ[1], 64, add)
                if dz == 2:
                    z_far(YZ, step)

            pl.when(place.active(dz))(go)
            if dz != 2:
                z_alone(YZ, step, dz // 2)

    def stage_c(step):
        z_near(YZ, step)

        def go():
            arrive_near(ZY, step)

            def add(tile):
                pb[step, 0, 1, tile, :] = (
                    pb[step, 0, 1, tile, :].astype(F32)
                    + zbz[step, 0, 1, tile, :].astype(F32)
                    + zbz[step, 1, 1, tile, :].astype(F32)
                ).astype(BF16)

            row_tiles(ZY[1], 64, add)
            traffic.send(
                lambda: (
                    pb.at[step, 0, 1, pl.ds(ZY[0], ZY[1])], yrz.at[step], yz_s.at[step],
                    yz_r.at[step], place.device(dy=1),
                ),
                0,
            )

        pl.when(place.active(0))(go)

    def stage_d(step):
        t = place.chunk(*ARRIVAL[step])

        def go():
            arrive_near(YZ, step)
            traffic.arrive(yry.at[step, 0], y_s.at[step, 0], y_r.at[step, 0])
            traffic.arrive(yrz.at[step], yz_s.at[step], yz_r.at[step])

            def finish(low, yr, zb0, zb1):
                def add(tile):
                    mine = pl.ds(pl.multiple_of(tile.start + low, 16), tile.size)
                    here = pl.ds(pl.multiple_of(tile.start + low + t * 256, 16), tile.size)
                    qkv[here, :] = (
                        pb[step, 0, 0, mine, :].astype(F32)
                        + yr[tile, :].astype(F32)
                        + zb0[tile, :].astype(F32)
                        + zb1[tile, :].astype(F32)
                    ).astype(BF16)

                return add

            row_tiles(
                ZY[1], 64, finish(ZY[0], yrz.at[step], zbz.at[step, 0, 0], zbz.at[step, 1, 0])
            )
            row_tiles(
                YZ[1], 64, finish(YZ[0], yry.at[step, 0], zby.at[step, 0], zby.at[step, 1])
            )

        pl.when(place.active(0))(go)

    schedule(PROJECT_LAGS, (stage_a, stage_b, stage_c, stage_d))
    return out_load


def attend_all(
    place, traffic, out_load, qkv_ref, out_ref,
    wv, at, score, acc, cs, cr, pb, ca, xb, yr,
    t_s, t_r, c_s, c_r, a_s, a_r, b_s, b_r, y_s, y_r,
):
    core = place.core
    factor = 1.4426950408889634 / HEAD_DIM**0.5

    def head_columns(dz, dy):
        return pl.ds(pl.multiple_of(place.head(dz, dy) * 128, 128), 128)

    def piece(step, dz, dy):
        return at.at[step, :, head_columns(dz, dy)]

    def attend(step):
        t = place.chunk(*DEPART[step])
        last = t // 2
        query = qkv_ref[pl.ds(pl.multiple_of(t * 256, 256), 256), 0:128]

        def block(j):
            return pl.ds(pl.multiple_of(j * 512, 512), 512)

        def scores(j):
            return lax.dot_general(
                query, qkv_ref[block(j), 128:256], (((1,), (1,)), ((), ())),
                preferred_element_type=F32,
            )

        def fold(op, wide):
            return op(op(wide[:, :128], wide[:, 128:256]), op(wide[:, 256:384], wide[:, 384:]))

        def first(j, top):
            now = scores(j)
            score[:, block(j)] = now
            return jnp.maximum(top, fold(jnp.maximum, now))

        row = lax.broadcasted_iota(jnp.int32, (256, 512), 0)
        col = lax.broadcasted_iota(jnp.int32, (256, 512), 1)
        now = jnp.where(row + (t % 2) * 256 >= col, scores(last), F32(-1e30))
        score[:, block(last)] = now
        top = lax.fori_loop(0, last, first, fold(jnp.maximum, now))
        top = jnp.max(top, 1, keepdims=True)

        def second(j, state):
            low, mixed = state
            weight = jnp.exp2((score[:, block(j)] - top) * factor)
            low = low + fold(jnp.add, weight)
            mixed = mixed + jnp.dot(
                weight.astype(BF16), qkv_ref[block(j), 256:384], preferred_element_type=F32
            )
            return low, mixed

        zero = jnp.zeros((256, 128), F32)
        low, mixed = lax.fori_loop(0, last + 1, second, (zero, zero))
        at[step, :, head_columns(0, 0)] = (mixed / jnp.sum(low, 1, keepdims=True)).astype(BF16)

    spread = []

    def share(step, dz, dy, ez, ey):
        rz, ry = (dz - ez) % 4, (dy + ey) % 2
        count = sum(1 for s in spread if s == step)
        spread.append(step)
        traffic.send(
            lambda: (
                piece(step, dz, dy), piece(step, dz, dy), t_s.at[step, count],
                t_r.at[step, rz, ry], place.device(dz=ez, dy=ey),
            ),
            dz,
        )

    def receive(step, dz, dy):
        traffic.arrive(piece(step, dz, dy), t_s.at[step, 0], t_r.at[step, dz, dy])

    def relay(step):
        return 1 if (step // 2) % 2 == 0 else 3

    def stage_a(step):
        def go():
            attend(step)
            for ez, ey in ((1, 0), (3, 0), (0, 1)):
                share(step, 0, 0, ez, ey)

        pl.when(place.active(0))(go)

    def stage_b(step):
        onward = relay(step)
        if SPREAD_Z_FIRST[step]:
            for dz in (4 - onward, onward):

                def go(dz=dz):
                    receive(step, dz, 0)
                    if dz == 4 - onward:
                        share(step, dz, 0, onward, 0)
                    share(step, dz, 0, 0, 1)

                pl.when(place.active(dz))(go)
        else:

            def go():
                receive(step, 0, 1)
                for ez in (1, 3):
                    share(step, 0, 1, ez, 0)

            pl.when(place.active(0))(go)

    def stage_c(step):
        onward = relay(step)
        if SPREAD_Z_FIRST[step]:

            def go():
                receive(step, 2, 0)
                share(step, 2, 0, 0, 1)

            pl.when(place.active(2))(go)
        else:

            def go():
                for dy in range(2):
                    receive(step, 4 - onward, dy)
                    share(step, 4 - onward, dy, onward, 0)

            pl.when(place.active(4 - onward))(go)

    def stage_d(step):
        if step == 0:
            out_load.wait()
        for dz, dy in OTHERS:
            if SPREAD_Z_FIRST[step]:
                done = dy == 0
            else:
                done = dz == 4 - relay(step) or (dz, dy) == (0, 1)
            if not done:
                pl.when(place.active(dz))(functools.partial(receive, step, dz, dy))

        def half(which):
            return pl.ds(pl.multiple_of(which * 128, 128), 128)

        def tile(i, carry):
            columns = pl.ds(pl.multiple_of(i * 512, 512), 512)
            score[:, 0:512] = jnp.dot(at[step], wv[:, columns], preferred_element_type=F32)
            cs[step, :, columns] = score[half(1 - core), 0:512].astype(BF16)
            acc[step % 2, :, columns] = score[half(core), 0:512]
            return carry

        lax.fori_loop(0, 3, tile, 0)
        traffic.send(
            lambda: (cs.at[step], cr.at[step], c_s.at[step], c_r.at[step], place.device(dcore=1))
        )

    def stage_e(step):
        dx, dyh = DEPART[step]
        traffic.arrive(cr.at[step], c_s.at[step], c_r.at[step])
        way = {1: 0, 3: 1}.get(dx)
        if way is not None:
            traffic.arrive(ca.at[dyh, way], a_s.at[dyh, way], a_r.at[dyh, way])
        if dx == 0:
            for w in range(2):
                traffic.arrive(xb.at[dyh, w], b_s.at[dyh, w], b_r.at[dyh, w])
            if dyh == 0:
                traffic.arrive(yr, y_s, y_r)

        def combine(lo):
            def add(rows):
                here = pl.ds(pl.multiple_of(rows.start + lo * 64, 16), rows.size)
                now = acc[step % 2, here, :] + cr[step, here, :].astype(F32)
                if way is not None and lo == way:
                    now = now + ca[dyh, way, rows, :].astype(F32)
                if dx == 0:
                    now = now + xb[dyh, 0, here, :].astype(F32) + xb[dyh, 1, here, :].astype(F32)
                if (dx, dyh) == (0, 0):
                    out_ref[here, :] = (now + yr[here, :].astype(F32)).astype(BF16)
                else:
                    pb[dx, dyh, here, :] = now.astype(BF16)

            row_tiles(64, 32, add)

        combine(0)
        combine(1)
        if dx == 2:
            for w, hop in ((0, 1), (1, 3)):
                traffic.send(
                    lambda w=w, hop=hop: (
                        pb.at[2, dyh, pl.ds(w * 64, 64)], ca.at[dyh, w], a_s.at[dyh, w],
                        a_r.at[dyh, w], place.device(dx=hop),
                    )
                )
        elif way is not None:
            traffic.send(
                lambda: (
                    pb.at[dx, dyh], xb.at[dyh, way], b_s.at[dyh, way], b_r.at[dyh, way],
                    place.device(dx=dx),
                )
            )
        elif dyh == 1:
            traffic.send(lambda: (pb.at[0, 1], yr, y_s, y_r, place.device(dyh=1)))

    schedule(ATTEND_LAGS, (stage_a, stage_b, stage_c, stage_d, stage_e))


def block_kernel(act_ref, w_ref, wo_ref, out_ref, qkv, wov, *scratch):
    place = Place()
    traffic = Traffic(place)
    cut = len(PROJECT_SCRATCH)
    out_load = project(place, traffic, act_ref, w_ref, wo_ref, wov, qkv, *scratch[:cut])
    attend_all(place, traffic, out_load, qkv, out_ref, wov, *scratch[cut:])
    traffic.drain()


def dma(*shape):
    return pltpu.SemaphoreType.DMA(shape) if shape else pltpu.SemaphoreType.DMA


PROJECT_SCRATCH = (
    pltpu.VMEM((3, 1536, 768), BF16),
    pltpu.VMEM((4, 2, 2, 128, 1536), BF16),
    pltpu.VMEM((8, 4, 2, 256, 384), BF16),
    pltpu.VMEM((8, ZY[1], 384), BF16),
    pltpu.VMEM((8, 4, YZ[1], 384), BF16),
    pltpu.VMEM((8, 2, 2, ZY[2], 384), BF16),
    pltpu.VMEM((8, 2, YZ[2], 384), BF16),
    pltpu.VMEM((8, 2, 2, ZY[1], 384), BF16),
    pltpu.VMEM((8, 2, YZ[1], 384), BF16),
    pltpu.VMEM((8, 8, 128), F32),
    dma(4), dma(8), dma(8), dma(16), dma(4, 2, 2), dma(8), dma(8), dma(8, 4), dma(8, 4),
    dma(2, 8, 2), dma(2, 8, 2), dma(2, 8, 2, 2), dma(2, 8, 2, 2),
)
ATTEND_SCRATCH = (
    pltpu.VMEM((8, 256, 768), BF16),
    pltpu.VMEM((256, 2048), F32),
    pltpu.VMEM((2, 128, 1536), F32),
    pltpu.VMEM((8, 128, 1536), BF16),
    pltpu.VMEM((8, 128, 1536), BF16),
    pltpu.VMEM((4, 2, 128, 1536), BF16),
    pltpu.VMEM((2, 2, 64, 1536), BF16),
    pltpu.VMEM((2, 2, 128, 1536), BF16),
    pltpu.VMEM((128, 1536), BF16),
    dma(8, 8), dma(8, 4, 2), dma(8), dma(8),
    dma(2, 2), dma(2, 2), dma(2, 2), dma(2, 2), dma(), dma(),
)


def per_device(activations, qkv_weight, out_weight):
    return pl.pallas_call(
        block_kernel,
        out_shape=jax.ShapeDtypeStruct((128, 1536), BF16),
        in_specs=[
            pl.BlockSpec(memory_space=pltpu.VMEM),
            pl.BlockSpec(memory_space=pl.ANY),
            pl.BlockSpec(memory_space=pl.ANY),
        ],
        out_specs=pl.BlockSpec(memory_space=pltpu.VMEM),
        scratch_shapes=[
            pltpu.VMEM((2048, 384), BF16),
            pltpu.VMEM((768, 1536), BF16),
            *PROJECT_SCRATCH,
            *ATTEND_SCRATCH,
        ],
        compiler_params=pltpu.CompilerParams(
            collective_id=1, has_side_effects=True, vmem_limit_bytes=60 << 20
        ),
        name="block",
    )(activations, jnp.transpose(qkv_weight, (1, 0, 2)), out_weight)


def solution(mesh):
    in_specs = (P("col", "row"), P("row", None, "col"), P("col", "row"))
    return jax.shard_map(
        per_device, mesh=mesh, in_specs=in_specs, out_specs=P("col", "row"), check_vma=False
    )
```
